256 devices in a mesh: gx: 8 (over x_lo, y), gy: 4 (over x_hi, core), gz: 8 (over z).
Axes of the slice: x: 4 (x_hi: 2, x_lo: 2; x = x_hi * 2 + x_lo), y: 4, z: 8, core: 2. Of those that a mesh axis runs over, the one named last changes fastest.
Arguments:
- tokens: bfloat16 [4096, 6144], P(('gx', 'gy'), 'gz'), may hold values from -6 to 6
- weight: bfloat16 [6144, 24576], P('gz', ('gy', 'gx')), may hold values from -0.15625 to 0.15625
- cotangent: bfloat16 [4096, 24576], P('gx', ('gy', 'gz')), may hold values from -0.5 to 0.5
Outputs:
- activated: bfloat16 [4096, 24576], P('gx', ('gy', 'gz'))
- input_grad: bfloat16 [4096, 6144], P(('gx', 'gy'), 'gz')
- weight_grad: bfloat16 [6144, 24576], P('gz', ('gy', 'gx'))
The draws below stay inside these ranges and needn't reach their ends.
All inputs are finite; a program needn't handle non-finite values.
Results may differ from the reference program's by a relative error of at most 0.023.
Values may be sent and summed in bfloat16 or wider, within the bound.
A program may use at most 128 MiB of HBM per device.

```python
import jax
import jax.numpy as jnp
from jax import lax

D = 6144
FF = 24576
TOK_DEV = 512
TOKENS = 4096
N_GX = 8


def strengthened(array, key, source, target, shards_of, factor):
    owner, partner = [(jnp.arange(array.shape[dim]) // (array.shape[dim] // shards_of)).reshape([-1 if axis == dim else 1 for axis in range(array.ndim)]) for dim in (source, target)]
    chosen = jax.random.permutation(key, shards_of)[partner]
    strong = (owner == chosen) | (owner == (partner + shards_of // 2) % shards_of)
    return jnp.where(strong, factor * array, array)


def levels(key, dims, cuts, low, largest):
    gain, own = 1.0, jax.random.fold_in(key, 6)
    for dim, blocks in cuts:
        heights = jnp.exp(jax.random.uniform(jax.random.fold_in(own, dim), (blocks,), jnp.float32, low / len(cuts), largest / len(cuts)))
        gain = gain * jnp.repeat(heights, dims[dim] // blocks).reshape([-1 if axis == dim else 1 for axis in range(len(dims))])
    return gain


def scatter_about(own_key, shape, width, most, cuts=(), dtype=jnp.bfloat16):
    drawn = jax.random.normal(own_key, shape, jnp.float32) * width
    if len(cuts) > 0:
        drawn = levels(own_key, shape, cuts, -0.22, 0.18) * drawn
    return jnp.clip(drawn, min=-most, max=most).astype(dtype)


def heavy_noise(rng, shape, spread, bound, cuts, heavy, held_as=jnp.bfloat16):
    result = spread * jax.random.normal(rng, shape, jnp.float32)
    if cuts:
        result = result * levels(rng, shape, cuts, -0.22, 0.18)
    return jnp.clip(strengthened(result, jax.random.fold_in(rng, 3), *heavy), -bound, bound).astype(held_as)


def setup_inputs(seed: int = 0) -> dict:
    splits = jax.random.split(jax.random.key(seed), 4)
    tokens = scatter_about(splits[0], (TOKENS, D), 1.0, 6.0, ((0, 32), (1, 8)))
    weight = heavy_noise(splits[1], (D, FF), D ** -0.5, 0.15625, ((0, 8), (1, 32)), (0, 1, 32, 2.75))
    cotangent = heavy_noise(splits[2], (TOKENS, FF), (TOKENS // 8) ** -0.5, 0.5, ((0, 8), (1, 32)), (0, 1, 32, 2.75))
    return {"tokens": tokens, "weight": weight, "cotangent": cotangent}


inv_root_two = 0.7071067811865476
inv_root_tau = 0.3989422804014327


def gelu_value(preact):
    return 0.5 * preact * (1.0 + jax.scipy.special.erf(preact * inv_root_two))


def gelu_slope(preact):
    return 0.5 * (1.0 + jax.scipy.special.erf(preact * inv_root_two)) + preact * jnp.exp(-0.5 * preact * preact) * inv_root_tau


def reference(tokens, weight, cotangent):
    preact = jnp.dot(tokens, weight, preferred_element_type=jnp.float32)
    activated = gelu_value(preact).astype(jnp.bfloat16)
    grad_pre = (cotangent.astype(jnp.float32) * gelu_slope(preact)).astype(jnp.bfloat16)
    input_grad = jnp.dot(grad_pre, weight.T, preferred_element_type=jnp.float32).astype(jnp.bfloat16)
    token_groups = tokens.reshape(N_GX, TOK_DEV, D)
    grad_groups = grad_pre.reshape(N_GX, TOK_DEV, FF)

    def add_group(total, pair):
        part_g = jnp.dot(pair[0].T, pair[1], preferred_element_type=jnp.float32).astype(jnp.bfloat16)
        part_g = lax.optimization_barrier(part_g)
        return total + part_g.astype(jnp.float32), None

    total, unused = lax.scan(add_group, jnp.zeros((D, FF), jnp.float32), (token_groups, grad_groups))
    return activated, input_grad, total.astype(jnp.bfloat16)
```

```python
import jax
import jax.numpy as jnp
from jax import lax
from jax.sharding import PartitionSpec as P

inv_root_two = 0.7071067811865476
inv_root_tau = 0.3989422804014327


def gelu_value(preact):
    return 0.5 * preact * (1.0 + jax.scipy.special.erf(preact * inv_root_two))


def gelu_slope(preact):
    return (
        0.5 * (1.0 + jax.scipy.special.erf(preact * inv_root_two))
        + preact * jnp.exp(-0.5 * preact * preact) * inv_root_tau
    )


def on_device(tokens, weight, cotangent):
    n = lax.axis_size("gz")
    swap = [(a * n + b, b * n + a) for a in range(n) for b in range(n)]
    token_rows = lax.all_gather(tokens, ("gx", "gy"), axis=0, tiled=True)
    cot = lax.ppermute(cotangent, ("gx", "gz"), swap)
    partial_value = jnp.dot(token_rows, weight, preferred_element_type=jnp.float32)
    preact = lax.psum_scatter(
        partial_value.astype(jnp.bfloat16), "gz", scatter_dimension=0, tiled=True
    ).astype(jnp.float32)
    activated = gelu_value(preact).astype(jnp.bfloat16)
    grad_pre = (cot.astype(jnp.float32) * gelu_slope(preact)).astype(jnp.bfloat16)
    activated = lax.ppermute(activated, ("gx", "gz"), swap)
    grads = lax.all_gather(grad_pre, "gz", axis=0, tiled=True)
    input_grad = lax.psum_scatter(
        lax.dot_general(
            grads, weight, (((1,), (1,)), ((), ())), preferred_element_type=jnp.float32
        ).astype(jnp.bfloat16),
        ("gx", "gy"),
        scatter_dimension=0,
        tiled=True,
    )
    weight_grad = lax.dot_general(
        token_rows, grads, (((0,), (0,)), ((), ())), preferred_element_type=jnp.float32
    ).astype(jnp.bfloat16)
    return (activated, input_grad, weight_grad)


def solution(mesh):
    in_specs = (P(("gx", "gy"), "gz"), P("gz", ("gy", "gx")), P("gx", ("gy", "gz")))
    out_specs = (P("gx", ("gy", "gz")), P(("gx", "gy"), "gz"), P("gz", ("gy", "gx")))
    return jax.shard_map(
        on_device, mesh=mesh, in_specs=in_specs, out_specs=out_specs, check_vma=False
    )
```

```python
import functools

import jax
import jax.numpy as jnp
from jax import lax
from jax.experimental import pallas as pl
from jax.experimental.pallas import tpu as pltpu
from jax.sharding import PartitionSpec as P

MESH = pl.DeviceIdType.MESH
inv_root_two = 0.7071067811865476
inv_root_tau = 0.3989422804014327

ORDER = (4, 3, 5, 2, 6, 1, 7, 0)
CHUNKS = 4


def plus(a, c):
    return lax.rem(lax.div(a, 4) + lax.div(c, 4), 2) * 4 + lax.rem(a + c, 4)


def minus(a, c):
    return lax.rem(lax.div(a, 4) - lax.div(c, 4) + 2, 2) * 4 + lax.rem(
        lax.rem(a, 4) - lax.rem(c, 4) + 4, 4
    )


def kernel(
    tok_ref, w_ref, cot_ref,
    act_ref, ig_ref, wg_ref,
    tokens, cot, given, taken, grads, act, total, near_out, near_in, far_out, far_in,
    t_send, t_recv, s_send, s_recv, c_send, c_recv, v_send, v_recv,
    r_send, r_recv, g_send, g_recv, n_send, n_recv, f_send, f_recv,
):
    a, q, b = lax.axis_index("gx"), lax.axis_index("gy"), lax.axis_index("gz")
    half, core = lax.div(q, 2), lax.rem(q, 2)
    piece = tok_ref.shape[0]
    rows = lambda r: pl.ds(pl.multiple_of(r * piece, piece), piece)
    at = lambda gx=a, gy=q, gz=b: {"gx": gx, "gy": gy, "gz": gz}
    up, down = lax.rem(b + 1, 8), lax.rem(b + 7, 8)
    sibling = at(gy=half * 2 + 1 - core)
    ahead = at(gx=a, gz=up), at(gx=a, gz=down)
    home = at(gx=plus(a, b), gz=a)
    source = at(gx=b, gz=minus(a, b))
    fixed = jnp.logical_and(a == 0, b == 0)
    moved = jnp.logical_not(fixed)
    offset = [lax.rem(b + o, 8) for o in ORDER]
    group = [plus(a, c) for c in offset]

    def remote(src, dst, send, recv, device):
        return pltpu.make_async_remote_copy(
            src_ref=src, dst_ref=dst, send_sem=send, recv_sem=recv, device_id=device, device_id_type=MESH
        )

    barrier = pltpu.get_barrier_semaphore()

    def greet(device):
        pl.semaphore_signal(barrier, inc=1, device_id=device, device_id_type=MESH)

    greet(at(gy=(1 - half) * 2 + core))
    greet(sibling)
    greet(ahead[0])
    greet(ahead[1])
    for c in range(1, 8):
        for j in range(2):
            greet(at(gx=plus(a, c), gy=j * 2 + core))

    @pl.when(moved)
    def _():
        greet(home)
        greet(source)

    pl.semaphore_wait(barrier, jnp.where(fixed, 18, 20))

    def token_copy(n, j):
        return remote(
            tok_ref, tokens.at[a, rows(q)], t_send.at[n * 2 + j], t_recv.at[n * 2 + half],
            at(gx=minus(a, offset[n]), gy=j * 2 + core),
        )

    def own(n, j):
        return jnp.logical_and(offset[n] == 0, half == j)

    def send_tokens(n):
        for j in range(2):

            @pl.when(jnp.logical_not(own(n, j)))
            def _():
                token_copy(n, j).start()

    def pass_copy(n, j, of):
        slot = tokens.at[group[n], rows(j * 2 + of)]
        return remote(slot, slot, s_send.at[n * 2 + j], s_recv.at[n * 2 + j], sibling)

    def get_tokens(n):
        for j in range(2):
            slot = tokens.at[group[n], rows(j * 2 + core)]

            @pl.when(jnp.logical_not(own(n, j)))
            def _():
                remote(slot, slot, t_send.at[n * 2 + j], t_recv.at[n * 2 + j], sibling).wait_recv()

            pass_copy(n, j, core).start()

    def get_passed(n):
        for j in range(2):
            pass_copy(n, j, 1 - core).wait_recv()

    def product(n, r):
        return jnp.dot(tokens[group[n], rows(r), :], w_ref[...], preferred_element_type=jnp.float32)

    def sum_copy(d, i):
        return remote(given.at[d, i], taken.at[d, i], r_send.at[d, i], r_recv.at[d, i], ahead[d])

    def place(d, p):
        return lax.rem(p + CHUNKS // 2, CHUNKS) if d == 0 else p

    def reduce_steps(first, last, base, n, add):
        def step(p, carry):
            i = base + p
            for d in range(2):
                value = product(n[d], place(d, p))
                if add:
                    sum_copy(d, i - CHUNKS).wait_recv()
                    value = value + taken[d, i - CHUNKS].astype(jnp.float32)
                given[d, i] = value.astype(jnp.bfloat16)
                sum_copy(d, i).start()
            return carry

        lax.fori_loop(first, last, step, 0)

    send_tokens(0)
    tokens[a, rows(q), :] = tok_ref[...]
    get_tokens(0)
    send_tokens(1)
    send_tokens(2)
    get_passed(0)

    cot_copy = remote(cot_ref, cot, c_send, c_recv, source)

    reduce_steps(2, 4, -2, (0, 0), False)

    @pl.when(moved)
    def _():
        cot_copy.start()

    @pl.when(fixed)
    def _():
        cot[...] = cot_ref[...]

    for k in (3, 2, 1):
        n = 7 - 2 * k
        get_tokens(n)
        get_tokens(n + 1)
        send_tokens(n + 2)
        if k > 1:
            send_tokens(n + 3)
        get_passed(n)
        get_passed(n + 1)
        base = (4 - k) * CHUNKS - 2
        if k == 3:
            reduce_steps(0, 2, base, (n, n + 1), False)
            reduce_steps(2, 4, base, (n, n + 1), True)
        else:
            reduce_steps(0, 4, base, (n, n + 1), True)
    get_tokens(7)
    get_passed(7)

    def own_product(r, carry):
        total[rows(r), :] = product(7, r)
        return carry

    lax.fori_loop(0, CHUNKS, own_product, 0)

    @pl.when(moved)
    def _():
        cot_copy.wait_recv()

    def grad_copy(d, u):
        k, p = lax.div(u, CHUNKS), lax.rem(u, CHUNKS)
        t = plus(a, lax.rem(b + 8 - k, 8) if d == 0 else lax.rem(b + k, 8))
        slot = grads.at[t, rows(p if d == 0 else lax.rem(p + CHUNKS // 2, CHUNKS))]
        return remote(slot, slot, g_send.at[d, u], g_recv.at[d, u], ahead[d])

    def grad_arrival(d, u):
        k, p = lax.div(u, CHUNKS) + 1, lax.rem(u, CHUNKS)
        t = plus(a, lax.rem(b + 8 - k, 8) if d == 0 else lax.rem(b + k, 8))
        slot = grads.at[t, rows(p if d == 0 else lax.rem(p + CHUNKS // 2, CHUNKS))]
        remote(slot, slot, g_send.at[d, u], g_recv.at[d, u], ahead[d]).wait_recv()

    def gelu_step(s, carry):
        r = lax.div(s, 2) + lax.rem(s, 2) * 2
        left = 10 + r
        right = 10 + lax.rem(r + 2, CHUNKS)
        sum_copy(0, right).wait_recv()
        sum_copy(1, left).wait_recv()
        x = total[rows(r), :] + taken[0, right].astype(jnp.float32) + taken[1, left].astype(jnp.float32)
        phi = 0.5 * (1.0 + lax.erf(x * inv_root_two))
        slope = phi + x * jnp.exp(-0.5 * x * x) * inv_root_tau
        act[rows(r), :] = (x * phi).astype(jnp.bfloat16)
        grads[group[7], rows(r), :] = (cot[rows(r), :].astype(jnp.float32) * slope).astype(jnp.bfloat16)
        grad_copy(0, r).start()
        grad_copy(1, lax.rem(r + 2, CHUNKS)).start()
        return carry

    lax.fori_loop(0, CHUNKS, gelu_step, 0)

    act_copy = remote(act, act_ref, v_send, v_recv, home)

    @pl.when(moved)
    def _():
        act_copy.start()

    @pl.when(fixed)
    def _():
        act_ref[...] = act[...]

    def near_copy(z, h):
        return remote(near_out.at[z * 2 + h], near_in.at[z * 2 + h], n_send.at[z * 2 + h], n_recv.at[z * 2 + h], sibling)

    def far_copy(z, h):
        return remote(
            far_out.at[z * 2 + h], far_in.at[z * 2 + half], f_send.at[z * 2 + h], f_recv.at[z * 2 + half],
            at(gx=plus(a, z), gy=h * 2 + core),
        )

    def far_own(z, h):
        return jnp.logical_and(z == 0, half == h)

    def back(t, r):
        return lax.dot_general(
            grads[t, rows(r), :], w_ref[...], (((1,), (1,)), ((), ())), preferred_element_type=jnp.float32
        )

    def give_near(z):
        def step(h, carry):
            near_out[z * 2 + h] = back(plus(a, z), h * 2 + 1 - core).astype(jnp.bfloat16)
            near_copy(z, h).start()
            return carry

        lax.fori_loop(0, 2, step, 0)

    def weigh(z, first=False):
        t = plus(a, z)

        def step(i, carry):
            columns = pl.ds(pl.multiple_of(i * 256, 256), 256)
            part = lax.dot_general(
                tokens[t, :, columns], grads[t], (((0,), (0,)), ((), ())), preferred_element_type=jnp.float32
            )
            total[columns, :] = part if first else total[columns, :] + part
            return carry

        lax.fori_loop(0, 3, step, 0)

    def give_far(z):
        def step(h, carry):
            value = back(plus(a, z), h * 2 + core)
            near_copy(z, h).wait_recv()
            value = (value + near_in[z * 2 + h].astype(jnp.float32)).astype(jnp.bfloat16)

            @pl.when(far_own(z, h))
            def _():
                far_in[z * 2 + half] = value

            @pl.when(jnp.logical_not(far_own(z, h)))
            def _():
                far_out[z * 2 + h] = value
                far_copy(z, h).start()

            return carry

        lax.fori_loop(0, 2, step, 0)

    give_near(b)
    weigh(b, True)
    give_far(b)
    for k in (1, 2, 3):

        def forward(p, carry):
            for d in range(2):
                grad_arrival(d, (k - 1) * CHUNKS + p)
                grad_copy(d, k * CHUNKS + p).start()
            return carry

        def keep(p, carry):
            for d in range(2):
                grad_arrival(d, (k - 1) * CHUNKS + p)
            return carry

        sent = CHUNKS if k < 3 else CHUNKS // 2
        lax.fori_loop(0, sent, forward, 0)
        lax.fori_loop(sent, CHUNKS, keep, 0)
        sides = lax.rem(b + 8 - k, 8), lax.rem(b + k, 8)
        for z in sides:
            give_near(z)
        for z in sides:
            weigh(z)
            give_far(z)

    def keep_last(p, carry):
        for d in range(2):
            grad_arrival(d, 3 * CHUNKS + p)
        return carry

    lax.fori_loop(0, CHUNKS // 2, keep_last, 0)
    opposite = lax.rem(b + 4, 8)
    give_near(opposite)
    give_far(opposite)
    weigh(opposite)

    def round_weight(i, carry):
        r = pl.ds(pl.multiple_of(i * 128, 128), 128)
        wg_ref[r, :] = total[r, :].astype(jnp.bfloat16)
        return carry

    lax.fori_loop(0, 6, round_weight, 0)

    def far_arrival(z, j):
        @pl.when(jnp.logical_not(far_own(z, j)))
        def _():
            slot = z * 2 + j
            remote(far_out.at[slot], far_in.at[slot], f_send.at[slot], f_recv.at[slot], sibling).wait_recv()

    def arrivals(z, carry):
        far_arrival(z, 0)
        far_arrival(z, 1)
        return carry

    lax.fori_loop(0, 8, arrivals, 0)

    def add_up(i, carry):
        r = pl.ds(pl.multiple_of(i * 16, 16), 16)
        value = far_in[0, r, :].astype(jnp.float32)
        for s in range(1, 16):
            value = value + far_in[s, r, :].astype(jnp.float32)
        ig_ref[r, :] = value.astype(jnp.bfloat16)
        return carry

    lax.fori_loop(0, piece // 16, add_up, 0)

    @pl.when(moved)
    def _():
        cot_copy.wait_send()
        act_copy.wait()

    for n in range(8):
        for j in range(2):
            pass_copy(n, j, core).wait_send()

            @pl.when(jnp.logical_not(own(n, j)))
            def _():
                token_copy(n, j).wait_send()

    def sent_sums(i, carry):
        for d in range(2):
            sum_copy(d, i).wait_send()
            grad_copy(d, i).wait_send()
        return carry

    lax.fori_loop(0, 14, sent_sums, 0)

    def sent_parts(z, carry):
        for h in range(2):
            near_copy(z, h).wait_send()

            @pl.when(jnp.logical_not(far_own(z, h)))
            def _():
                far_copy(z, h).wait_send()

        return carry

    lax.fori_loop(0, 8, sent_parts, 0)


def on_device(tokens, weight, cotangent):
    (piece, depth), (group, units) = tokens.shape, cotangent.shape
    bf16 = jnp.bfloat16
    shape = jax.ShapeDtypeStruct
    vmem = pl.BlockSpec(memory_space=pltpu.VMEM)
    dma = pltpu.SemaphoreType.DMA
    return pl.pallas_call(
        kernel,
        out_shape=(shape(cotangent.shape, bf16), shape(tokens.shape, bf16), shape(weight.shape, bf16)),
        in_specs=[vmem] * 3,
        out_specs=(vmem,) * 3,
        scratch_shapes=[
            pltpu.VMEM((8, group, depth), bf16),
            pltpu.VMEM((group, units), bf16),
            pltpu.VMEM((2, 14, piece, units), bf16),
            pltpu.VMEM((2, 14, piece, units), bf16),
            pltpu.VMEM((8, group, units), bf16),
            pltpu.VMEM((group, units), bf16),
            pltpu.VMEM((depth, units), jnp.float32),
            pltpu.VMEM((16, piece, depth), bf16),
            pltpu.VMEM((16, piece, depth), bf16),
            pltpu.VMEM((16, piece, depth), bf16),
            pltpu.VMEM((16, piece, depth), bf16),
            dma((16,)), dma((16,)), dma((16,)), dma((16,)),
            dma, dma, dma, dma,
            dma((2, 14)), dma((2, 14)), dma((2, 14)), dma((2, 14)),
            dma((16,)), dma((16,)), dma((16,)), dma((16,)),
        ],
        compiler_params=pltpu.CompilerParams(
            collective_id=0, has_side_effects=True, vmem_limit_bytes=60 * 1024 * 1024
        ),
    )(tokens, weight, cotangent)


def solution(mesh):
    in_specs = (P(("gx", "gy"), "gz"), P("gz", ("gy", "gx")), P("gx", ("gy", "gz")))
    out_specs = (P("gx", ("gy", "gz")), P(("gx", "gy"), "gz"), P("gz", ("gy", "gx")))
    return jax.shard_map(
        on_device, mesh=mesh, in_specs=in_specs, out_specs=out_specs, check_vma=False
    )
```

```python
import functools

import jax
import jax.numpy as jnp
from jax import lax
from jax.experimental import pallas as pl
from jax.experimental.pallas import tpu as pltpu
from jax.sharding import PartitionSpec as P

MESH = pl.DeviceIdType.MESH
inv_root_two = 0.7071067811865476
inv_root_tau = 0.3989422804014327

LANDING = (
    (1, 3, 5, 2, 0, 7, 4, 6),
    (7, 2, 4, 3, 6, 1, 5, 0),
    (6, 4, 2, 0, 7, 5, 1, 3),
    (2, 7, 6, 1, 4, 3, 0, 5),
    (0, 5, 3, 6, 1, 4, 7, 2),
    (3, 1, 0, 7, 5, 2, 6, 4),
    (5, 0, 1, 4, 3, 6, 2, 7),
    (4, 6, 7, 5, 2, 0, 3, 1),
)
Z_OF = tuple(tuple(LANDING[a].index(t) for t in range(8)) for a in range(8))
UNITS_OF = tuple(tuple([row[b] for row in LANDING].index(t) for b in range(8)) for t in range(8))
ORDER = (4, 3, 5, 2, 6, 1, 7, 0)
CHUNKS = 4


def choose(values, i):
    value = values[0]
    for k in range(1, len(values)):
        value = jnp.where(i == k, values[k], value)
    return value


def row_of(table, i):
    return choose([sum(v * 8**k for k, v in enumerate(row)) for row in table], i)


def entry(row, k):
    return lax.rem(lax.div(row, choose([8**p for p in range(8)], k)), 8)


def kernel(
    tok_ref, w_ref, cot_ref,
    act_ref, ig_ref, wg_ref,
    tokens, cot, cot_mid, act_mid, given, taken, grads, act, total, near_out, near_in, far_out, far_in,
    t_send, t_recv, s_send, s_recv, m_send, m_recv,
    r_send, r_recv, g_send, g_recv, n_send, n_recv, f_send, f_recv,
):
    a, q, b = lax.axis_index("gx"), lax.axis_index("gy"), lax.axis_index("gz")
    half, core = lax.div(q, 2), lax.rem(q, 2)
    piece = tok_ref.shape[0]
    rows = lambda r: pl.ds(pl.multiple_of(r * piece, piece), piece)
    at = lambda gx=a, gy=q, gz=b: {"gx": gx, "gy": gy, "gz": gz}
    up, down = lax.rem(b + 1, 8), lax.rem(b + 7, 8)
    sibling = at(gy=half * 2 + 1 - core)
    ahead = at(gx=a, gz=up), at(gx=a, gz=down)
    landings = row_of(LANDING, a)
    land = lambda z: entry(landings, z)
    units = entry(row_of(UNITS_OF, a), b)
    place_z = entry(row_of(Z_OF, b), a)
    turned, shifted = place_z != b, units != a
    x, y = half * 2 + lax.div(a, 4), lax.rem(a, 4)
    offset = [lax.rem(b + o, 8) for o in ORDER]
    group = [land(c) for c in offset]

    def remote(src, dst, send, recv, device):
        return pltpu.make_async_remote_copy(
            src_ref=src, dst_ref=dst, send_sem=send, recv_sem=recv, device_id=device, device_id_type=MESH
        )

    barrier = pltpu.get_barrier_semaphore()

    def greet(device):
        pl.semaphore_signal(barrier, inc=1, device_id=device, device_id_type=MESH)

    greet(at(gy=(1 - half) * 2 + core))
    greet(sibling)
    greet(ahead[0])
    greet(ahead[1])
    for c in range(1, 8):
        for j in range(2):
            greet(at(gx=lax.rem(a + c, 8), gy=j * 2 + core))

    @pl.when(turned)
    def _():
        greet(at(gz=place_z))
        greet(at(gz=units))

    pl.semaphore_wait(barrier, jnp.where(turned, 20, 18))

    side = piece // 2

    def spot(i, j, s, lo=0, n=side, of=core):
        px, py = lax.rem(x + i, 4), lax.rem(y + j, 4)
        row = (lax.div(px, 2) * 2 + of) * piece + s * side + lo
        return tokens.at[lax.rem(px, 2) * 4 + py, pl.ds(pl.multiple_of(row, side // 2), n)]

    def chip(i, j):
        px, py = lax.rem(x + i, 4), lax.rem(y + j, 4)
        return at(gx=lax.rem(px, 2) * 4 + py, gy=lax.div(px, 2) * 2 + core)

    def from_whom(w):
        return 1 if w in (0, 3) else 3

    def what(w):
        return ((1, 0, side), (3, 0, side), (2, 0, side // 2), (2, side // 2, side // 2))[w]

    def first_copy(s, w, arrival):
        e, lo, n = what(w)
        to = 4 - from_whom(w)
        if not arrival:
            e = (e + to) % 4
        slot = spot(e, 0, s, lo, n) if s == 0 else spot(0, e, s, lo, n)
        i = s * 4 + w
        return remote(slot, slot, t_send.at[i], t_recv.at[i], chip(to, 0) if s == 0 else chip(0, to))

    def second_copy(s, e, w, arrival):
        f, lo, n = what(w)
        to = 4 - from_whom(w)
        if not arrival:
            f = (f + to) % 4
        slot = spot(e, f, s, lo, n) if s == 0 else spot(f, e, s, lo, n)
        i = 8 + s * 16 + e * 4 + w
        return remote(slot, slot, t_send.at[i], t_recv.at[i], chip(0, to) if s == 0 else chip(to, 0))

    def pass_copy(s, e, f, of):
        slot = spot(e, f, s, of=of) if s == 0 else spot(f, e, s, of=of)
        i = s * 16 + e * 4 + f
        return remote(slot, slot, s_send.at[i], s_recv.at[i], sibling)

    def give_second(e):
        for s in range(2):
            second_copy(s, e, 0, False).start()
            second_copy(s, e, 1, False).start()
            pass_copy(s, e, 0, core).start()

    def relay_second(e):
        for s in range(2):
            for w in range(2):
                second_copy(s, e, w, True).wait_recv()
                second_copy(s, e, 3 - w, False).start()
                pass_copy(s, e, 1 + 2 * w, core).start()

    def end_second(e):
        for s in range(2):
            second_copy(s, e, 2, True).wait_recv()
            second_copy(s, e, 3, True).wait_recv()
            pass_copy(s, e, 2, core).start()

    def gather_tokens():
        tokens[a, rows(q), :] = tok_ref[...]
        for s in range(2):
            first_copy(s, 0, False).start()
            first_copy(s, 1, False).start()
        give_second(0)
        for w in range(2):
            for s in range(2):
                first_copy(s, w, True).wait_recv()
                first_copy(s, 3 - w, False).start()
            give_second(1 + 2 * w)
        relay_second(0)
        for s in range(2):
            first_copy(s, 2, True).wait_recv()
            first_copy(s, 3, True).wait_recv()
        give_second(2)
        for e in (1, 3):
            relay_second(e)
        end_second(0)
        relay_second(2)
        for e in (1, 3, 2):
            end_second(e)
        for s in range(2):
            for e in range(4):
                for f in range(4):
                    pass_copy(s, e, f, 1 - core).wait_recv()

    cot_turn = remote(cot_ref, cot_mid, m_send.at[0], m_recv.at[0], at(gz=place_z))
    cot_shift = remote(cot_mid, cot, m_send.at[1], m_recv.at[1], at(gx=units))

    def act_shift(r):
        return remote(act.at[rows(r)], act_mid.at[rows(r)], m_send.at[2 + r], m_recv.at[2 + r], at(gx=land(b)))

    def act_turn(r):
        return remote(act_mid.at[rows(r)], act_ref.at[rows(r)], m_send.at[6 + r], m_recv.at[6 + r], at(gz=units))

    def set_off(copy, leaves, src, dst, r=slice(None)):
        @pl.when(leaves)
        def _():
            copy.start()

        @pl.when(jnp.logical_not(leaves))
        def _():
            dst[r, :] = src[r, :]

    def arrived(copy, leaves):
        @pl.when(leaves)
        def _():
            copy.wait_recv()

    def departed(copy, leaves):
        @pl.when(leaves)
        def _():
            copy.wait_send()

    def product(n, r):
        return jnp.dot(tokens[group[n], rows(r), :], w_ref[...], preferred_element_type=jnp.float32)

    def sum_copy(d, i):
        return remote(given.at[d, i], taken.at[d, i], r_send.at[d, i], r_recv.at[d, i], ahead[d])

    def place(d, p):
        return lax.rem(p + CHUNKS // 2, CHUNKS) if d == 0 else p

    def reduce_steps(first, last, base, n, add):
        def step(p, carry):
            i = base + p
            for d in range(2):
                value = product(n[d], place(d, p))
                if add:
                    sum_copy(d, i - CHUNKS).wait_recv()
                    value = value + taken[d, i - CHUNKS].astype(jnp.float32)
                given[d, i] = value.astype(jnp.bfloat16)
                sum_copy(d, i).start()
            return carry

        lax.fori_loop(first, last, step, 0)

    set_off(cot_turn, turned, cot_ref, cot_mid)
    gather_tokens()
    reduce_steps(2, 4, -2, (0, 0), False)
    arrived(cot_turn, turned)
    set_off(cot_shift, shifted, cot_mid, cot)
    for k in (3, 2, 1):
        n = 7 - 2 * k
        base = (4 - k) * CHUNKS - 2
        if k == 3:
            reduce_steps(0, 2, base, (n, n + 1), False)
            reduce_steps(2, 4, base, (n, n + 1), True)
        else:
            reduce_steps(0, 4, base, (n, n + 1), True)

    def own_product(r, carry):
        total[rows(r), :] = product(7, r)
        return carry

    lax.fori_loop(0, CHUNKS, own_product, 0)

    arrived(cot_shift, shifted)

    def grad_copy(d, u):
        k, p = lax.div(u, CHUNKS), lax.rem(u, CHUNKS)
        t = land(lax.rem(b + 8 - k, 8) if d == 0 else lax.rem(b + k, 8))
        slot = grads.at[t, rows(p if d == 0 else lax.rem(p + CHUNKS // 2, CHUNKS))]
        return remote(slot, slot, g_send.at[d, u], g_recv.at[d, u], ahead[d])

    def grad_arrival(d, u):
        k, p = lax.div(u, CHUNKS) + 1, lax.rem(u, CHUNKS)
        t = land(lax.rem(b + 8 - k, 8) if d == 0 else lax.rem(b + k, 8))
        slot = grads.at[t, rows(p if d == 0 else lax.rem(p + CHUNKS // 2, CHUNKS))]
        remote(slot, slot, g_send.at[d, u], g_recv.at[d, u], ahead[d]).wait_recv()

    def gelu_step(s, carry):
        r = lax.div(s, 2) + lax.rem(s, 2) * 2
        left = 10 + r
        right = 10 + lax.rem(r + 2, CHUNKS)
        sum_copy(0, right).wait_recv()
        sum_copy(1, left).wait_recv()
        x = total[rows(r), :] + taken[0, right].astype(jnp.float32) + taken[1, left].astype(jnp.float32)
        phi = 0.5 * (1.0 + lax.erf(x * inv_root_two))
        slope = phi + x * jnp.exp(-0.5 * x * x) * inv_root_tau
        act[rows(r), :] = (x * phi).astype(jnp.bfloat16)
        grads[group[7], rows(r), :] = (cot[rows(r), :].astype(jnp.float32) * slope).astype(jnp.bfloat16)
        grad_copy(0, r).start()
        grad_copy(1, lax.rem(r + 2, CHUNKS)).start()
        set_off(act_shift(r), shifted, act, act_mid, rows(r))
        return carry

    lax.fori_loop(0, CHUNKS, gelu_step, 0)

    def near_copy(z, h):
        return remote(near_out.at[z * 2 + h], near_in.at[z * 2 + h], n_send.at[z * 2 + h], n_recv.at[z * 2 + h], sibling)

    def far_copy(z, h):
        return remote(
            far_out.at[z * 2 + h], far_in.at[z * 2 + half], f_send.at[z * 2 + h], f_recv.at[z * 2 + half],
            at(gx=land(z), gy=h * 2 + core),
        )

    def far_own(z, h):
        return jnp.logical_and(land(z) == a, half == h)

    def back(t, r):
        return lax.dot_general(
            grads[t, rows(r), :], w_ref[...], (((1,), (1,)), ((), ())), preferred_element_type=jnp.float32
        )

    def give_near(z):
        def step(h, carry):
            near_out[z * 2 + h] = back(land(z), h * 2 + 1 - core).astype(jnp.bfloat16)
            near_copy(z, h).start()
            return carry

        lax.fori_loop(0, 2, step, 0)

    def weigh(z, first=False):
        t = land(z)

        def step(i, carry):
            columns = pl.ds(pl.multiple_of(i * 256, 256), 256)
            part = lax.dot_general(
                tokens[t, :, columns], grads[t], (((0,), (0,)), ((), ())), preferred_element_type=jnp.float32
            )
            total[columns, :] = part if first else total[columns, :] + part
            return carry

        lax.fori_loop(0, 3, step, 0)

    def give_far(z):
        def step(h, carry):
            value = back(land(z), h * 2 + core)
            near_copy(z, h).wait_recv()
            value = (value + near_in[z * 2 + h].astype(jnp.float32)).astype(jnp.bfloat16)

            @pl.when(far_own(z, h))
            def _():
                far_in[z * 2 + half] = value

            @pl.when(jnp.logical_not(far_own(z, h)))
            def _():
                far_out[z * 2 + h] = value
                far_copy(z, h).start()

            return carry

        lax.fori_loop(0, 2, step, 0)

    give_near(b)
    weigh(b, True)
    give_far(b)
    for k in (1, 2, 3):

        def forward(p, carry):
            for d in range(2):
                grad_arrival(d, (k - 1) * CHUNKS + p)
                grad_copy(d, k * CHUNKS + p).start()
            if k == 2:
                arrived(act_shift(p), shifted)
                set_off(act_turn(p), turned, act_mid, act_ref, rows(p))
            return carry

        def keep(p, carry):
            for d in range(2):
                grad_arrival(d, (k - 1) * CHUNKS + p)
            return carry

        sent = CHUNKS if k < 3 else CHUNKS // 2
        lax.fori_loop(0, sent, forward, 0)
        lax.fori_loop(sent, CHUNKS, keep, 0)
        sides = lax.rem(b + 8 - k, 8), lax.rem(b + k, 8)
        for z in sides:
            give_near(z)
        for z in sides:
            weigh(z)
            give_far(z)

    def keep_last(p, carry):
        for d in range(2):
            grad_arrival(d, 3 * CHUNKS + p)
        return carry

    lax.fori_loop(0, CHUNKS // 2, keep_last, 0)
    opposite = lax.rem(b + 4, 8)
    give_near(opposite)
    give_far(opposite)
    weigh(opposite)

    def round_weight(i, carry):
        r = pl.ds(pl.multiple_of(i * 128, 128), 128)
        wg_ref[r, :] = total[r, :].astype(jnp.bfloat16)
        return carry

    lax.fori_loop(0, 6, round_weight, 0)

    def far_arrival(z, j):
        @pl.when(jnp.logical_not(far_own(z, j)))
        def _():
            slot = z * 2 + j
            remote(far_out.at[slot], far_in.at[slot], f_send.at[slot], f_recv.at[slot], sibling).wait_recv()

    def arrivals(z, carry):
        far_arrival(z, 0)
        far_arrival(z, 1)
        return carry

    lax.fori_loop(0, 8, arrivals, 0)

    def add_up(i, carry):
        r = pl.ds(pl.multiple_of(i * 16, 16), 16)
        value = far_in[0, r, :].astype(jnp.float32)
        for s in range(1, 16):
            value = value + far_in[s, r, :].astype(jnp.float32)
        ig_ref[r, :] = value.astype(jnp.bfloat16)
        return carry

    lax.fori_loop(0, piece // 16, add_up, 0)

    departed(cot_turn, turned)
    departed(cot_shift, shifted)
    for r in range(CHUNKS):
        arrived(act_turn(r), turned)
        departed(act_turn(r), turned)
        departed(act_shift(r), shifted)
    for s in range(2):
        for w in range(4):
            first_copy(s, w, False).wait_send()
        for e in range(4):
            for w in range(4):
                second_copy(s, e, w, False).wait_send()
                pass_copy(s, e, w, core).wait_send()

    def sent_sums(i, carry):
        for d in range(2):
            sum_copy(d, i).wait_send()
            grad_copy(d, i).wait_send()
        return carry

    lax.fori_loop(0, 14, sent_sums, 0)

    def sent_parts(z, carry):
        for h in range(2):
            near_copy(z, h).wait_send()

            @pl.when(jnp.logical_not(far_own(z, h)))
            def _():
                far_copy(z, h).wait_send()

        return carry

    lax.fori_loop(0, 8, sent_parts, 0)


def on_device(tokens, weight, cotangent):
    (piece, depth), (group, units) = tokens.shape, cotangent.shape
    bf16 = jnp.bfloat16
    shape = jax.ShapeDtypeStruct
    vmem = pl.BlockSpec(memory_space=pltpu.VMEM)
    dma = pltpu.SemaphoreType.DMA
    return pl.pallas_call(
        kernel,
        out_shape=(shape(cotangent.shape, bf16), shape(tokens.shape, bf16), shape(weight.shape, bf16)),
        in_specs=[vmem] * 3,
        out_specs=(vmem,) * 3,
        scratch_shapes=[
            pltpu.VMEM((8, group, depth), bf16),
            pltpu.VMEM((group, units), bf16),
            pltpu.VMEM((group, units), bf16),
            pltpu.VMEM((group, units), bf16),
            pltpu.VMEM((2, 14, piece, units), bf16),
            pltpu.VMEM((2, 14, piece, units), bf16),
            pltpu.VMEM((8, group, units), bf16),
            pltpu.VMEM((group, units), bf16),
            pltpu.VMEM((depth, units), jnp.float32),
            pltpu.VMEM((16, piece, depth), bf16),
            pltpu.VMEM((16, piece, depth), bf16),
            pltpu.VMEM((16, piece, depth), bf16),
            pltpu.VMEM((16, piece, depth), bf16),
            dma((40,)), dma((40,)), dma((32,)), dma((32,)),
            dma((10,)), dma((10,)),
            dma((2, 14)), dma((2, 14)), dma((2, 14)), dma((2, 14)),
            dma((16,)), dma((16,)), dma((16,)), dma((16,)),
        ],
        compiler_params=pltpu.CompilerParams(
            collective_id=0, has_side_effects=True, vmem_limit_bytes=60 * 1024 * 1024
        ),
    )(tokens, weight, cotangent)


def solution(mesh):
    in_specs = (P(("gx", "gy"), "gz"), P("gz", ("gy", "gx")), P("gx", ("gy", "gz")))
    out_specs = (P("gx", ("gy", "gz")), P(("gx", "gy"), "gz"), P("gz", ("gy", "gx")))
    return jax.shard_map(
        on_device, mesh=mesh, in_specs=in_specs, out_specs=out_specs, check_vma=False
    )
```

```python
import functools

import jax
import jax.numpy as jnp
from jax import lax
from jax.experimental import pallas as pl
from jax.experimental.pallas import tpu as pltpu
from jax.sharding import PartitionSpec as P

MESH = pl.DeviceIdType.MESH
inv_root_two = 0.7071067811865476
inv_root_tau = 0.3989422804014327

LANDING = (
    (2, 5, 4, 3, 6, 1, 0, 7),
    (1, 2, 7, 0, 5, 6, 3, 4),
    (0, 3, 6, 1, 4, 7, 2, 5),
    (7, 4, 5, 6, 3, 0, 1, 2),
    (6, 1, 0, 7, 2, 5, 4, 3),
    (5, 6, 3, 4, 1, 2, 7, 0),
    (4, 7, 2, 5, 0, 3, 6, 1),
    (3, 0, 1, 2, 7, 4, 5, 6),
)
Z_OF = tuple(tuple(LANDING[a].index(t) for t in range(8)) for a in range(8))
UNITS_OF = tuple(tuple([row[b] for row in LANDING].index(t) for b in range(8)) for t in range(8))
ORDER = (4, 3, 5, 2, 6, 1, 7, 0)
CHUNKS = 4


def choose(values, i):
    value = values[0]
    for k in range(1, len(values)):
        value = jnp.where(i == k, values[k], value)
    return value


def row_of(table, i):
    return choose([sum(v * 8**k for k, v in enumerate(row)) for row in table], i)


def entry(row, k):
    return lax.rem(lax.div(row, choose([8**p for p in range(8)], k)), 8)


def kernel(
    tok_ref, w_ref, cot_ref,
    act_ref, ig_ref, wg_ref,
    tokens, cot, cot_mid, act_mid, given, taken, grads, act, total, near_out, near_in, far_out, far_in,
    t_send, t_recv, s_send, s_recv, m_send, m_recv,
    r_send, r_recv, g_send, g_recv, n_send, n_recv, f_send, f_recv,
):
    a, q, b = lax.axis_index("gx"), lax.axis_index("gy"), lax.axis_index("gz")
    half, core = lax.div(q, 2), lax.rem(q, 2)
    piece = tok_ref.shape[0]
    rows = lambda r: pl.ds(pl.multiple_of(r * piece, piece), piece)
    at = lambda gx=a, gy=q, gz=b: {"gx": gx, "gy": gy, "gz": gz}
    up, down = lax.rem(b + 1, 8), lax.rem(b + 7, 8)
    sibling = at(gy=half * 2 + 1 - core)
    ahead = at(gx=a, gz=up), at(gx=a, gz=down)
    landings = row_of(LANDING, a)
    land = lambda z: entry(landings, z)
    units = entry(row_of(UNITS_OF, a), b)
    place_z = entry(row_of(Z_OF, b), a)
    turned, shifted = place_z != b, units != a
    x, y = half * 2 + lax.div(a, 4), lax.rem(a, 4)
    offset = [lax.rem(b + o, 8) for o in ORDER]
    group = [land(c) for c in offset]

    def remote(src, dst, send, recv, device):
        return pltpu.make_async_remote_copy(
            src_ref=src, dst_ref=dst, send_sem=send, recv_sem=recv, device_id=device, device_id_type=MESH
        )

    barrier = pltpu.get_barrier_semaphore()

    def greet(device):
        pl.semaphore_signal(barrier, inc=1, device_id=device, device_id_type=MESH)

    greet(at(gy=(1 - half) * 2 + core))
    greet(sibling)
    greet(ahead[0])
    greet(ahead[1])
    for c in range(1, 8):
        for j in range(2):
            greet(at(gx=lax.rem(a + c, 8), gy=j * 2 + core))

    @pl.when(turned)
    def _():
        greet(at(gz=place_z))
        greet(at(gz=units))

    pl.semaphore_wait(barrier, jnp.where(turned, 20, 18))

    side = piece // 2

    def spot(i, j, s, lo=0, n=side, of=core):
        px, py = lax.rem(x + i, 4), lax.rem(y + j, 4)
        row = (lax.div(px, 2) * 2 + of) * piece + s * side + lo
        return tokens.at[lax.rem(px, 2) * 4 + py, pl.ds(pl.multiple_of(row, side // 2), n)]

    def chip(i, j):
        px, py = lax.rem(x + i, 4), lax.rem(y + j, 4)
        return at(gx=lax.rem(px, 2) * 4 + py, gy=lax.div(px, 2) * 2 + core)

    def from_whom(w):
        return 1 if w in (0, 3) else 3

    def what(w):
        return ((1, 0, side), (3, 0, side), (2, 0, side // 2), (2, side // 2, side // 2))[w]

    def first_copy(s, w, arrival):
        e, lo, n = what(w)
        to = 4 - from_whom(w)
        if not arrival:
            e = (e + to) % 4
        slot = spot(e, 0, s, lo, n) if s == 0 else spot(0, e, s, lo, n)
        i = s * 4 + w
        return remote(slot, slot, t_send.at[i], t_recv.at[i], chip(to, 0) if s == 0 else chip(0, to))

    def second_copy(s, e, w, arrival):
        f, lo, n = what(w)
        to = 4 - from_whom(w)
        if not arrival:
            f = (f + to) % 4
        slot = spot(e, f, s, lo, n) if s == 0 else spot(f, e, s, lo, n)
        i = 8 + s * 16 + e * 4 + w
        return remote(slot, slot, t_send.at[i], t_recv.at[i], chip(0, to) if s == 0 else chip(to, 0))

    def pass_copy(s, e, f, of):
        slot = spot(e, f, s, of=of) if s == 0 else spot(f, e, s, of=of)
        i = s * 16 + e * 4 + f
        return remote(slot, slot, s_send.at[i], s_recv.at[i], sibling)

    def give_second(e):
        for s in range(2):
            second_copy(s, e, 0, False).start()
            second_copy(s, e, 1, False).start()
            pass_copy(s, e, 0, core).start()

    def relay_second(e):
        for s in range(2):
            for w in range(2):
                second_copy(s, e, w, True).wait_recv()
                second_copy(s, e, 3 - w, False).start()
                pass_copy(s, e, 1 + 2 * w, core).start()

    def end_second(e):
        for s in range(2):
            second_copy(s, e, 2, True).wait_recv()
            second_copy(s, e, 3, True).wait_recv()
            pass_copy(s, e, 2, core).start()

    cot_shift = remote(cot_mid, cot, m_send.at[1], m_recv.at[1], at(gx=units))

    def cot_turn(r):
        return remote(cot_ref.at[rows(r)], cot_mid.at[rows(r)], m_send.at[10 + r], m_recv.at[10 + r], at(gz=place_z))

    def act_shift(r):
        return remote(act.at[rows(r)], act_mid.at[rows(r)], m_send.at[2 + r], m_recv.at[2 + r], at(gx=land(b)))

    def act_turn(r):
        return remote(act_mid.at[rows(r)], act_ref.at[rows(r)], m_send.at[6 + r], m_recv.at[6 + r], at(gz=units))

    def set_off(copy, leaves, src, dst, r=slice(None)):
        @pl.when(leaves)
        def _():
            copy.start()

        @pl.when(jnp.logical_not(leaves))
        def _():
            dst[r, :] = src[r, :]

    def arrived(copy, leaves):
        @pl.when(leaves)
        def _():
            copy.wait_recv()

    def departed(copy, leaves):
        @pl.when(leaves)
        def _():
            copy.wait_send()

    def turn_act(r):
        arrived(act_shift(r), shifted)
        set_off(act_turn(r), turned, act_mid, act_ref, rows(r))

    def turn_cot(r):
        set_off(cot_turn(r), turned, cot_ref, cot_mid, rows(r))

    def gather_tokens():
        tokens[a, rows(q), :] = tok_ref[...]
        for s in range(2):
            first_copy(s, 0, False).start()
            first_copy(s, 1, False).start()
        give_second(0)
        turn_cot(0)
        for w in range(2):
            for s in range(2):
                first_copy(s, w, True).wait_recv()
                first_copy(s, 3 - w, False).start()
            give_second(1 + 2 * w)
            turn_cot(1 + w)
        relay_second(0)
        turn_cot(3)
        for s in range(2):
            first_copy(s, 2, True).wait_recv()
            first_copy(s, 3, True).wait_recv()
        give_second(2)
        for e in (1, 3):
            relay_second(e)
        end_second(0)
        relay_second(2)
        for e in (1, 3, 2):
            end_second(e)
        for s in range(2):
            for e in range(4):
                for f in range(4):
                    pass_copy(s, e, f, 1 - core).wait_recv()

    def product(n, r):
        return jnp.dot(tokens[group[n], rows(r), :], w_ref[...], preferred_element_type=jnp.float32)

    def sum_copy(d, i):
        return remote(given.at[d, i], taken.at[d, i], r_send.at[d, i], r_recv.at[d, i], ahead[d])

    def place(d, p):
        return lax.rem(p + CHUNKS // 2, CHUNKS) if d == 0 else p

    def reduce_steps(first, last, base, n, add):
        def step(p, carry):
            i = base + p
            for d in range(2):
                value = product(n[d], place(d, p))
                if add:
                    sum_copy(d, i - CHUNKS).wait_recv()
                    value = value + taken[d, i - CHUNKS].astype(jnp.float32)
                given[d, i] = value.astype(jnp.bfloat16)
                sum_copy(d, i).start()
            return carry

        lax.fori_loop(first, last, step, 0)

    gather_tokens()
    reduce_steps(2, 4, -2, (0, 0), False)
    for k in (3, 2, 1):
        if k == 2:
            for r in range(CHUNKS):
                arrived(cot_turn(r), turned)
            set_off(cot_shift, shifted, cot_mid, cot)
        n = 7 - 2 * k
        base = (4 - k) * CHUNKS - 2
        if k == 3:
            reduce_steps(0, 2, base, (n, n + 1), False)
            reduce_steps(2, 4, base, (n, n + 1), True)
        else:
            reduce_steps(0, 4, base, (n, n + 1), True)

    def own_product(r, carry):
        total[rows(r), :] = product(7, r)
        return carry

    lax.fori_loop(0, CHUNKS, own_product, 0)

    arrived(cot_shift, shifted)

    def grad_copy(d, u):
        k, p = lax.div(u, CHUNKS), lax.rem(u, CHUNKS)
        t = land(lax.rem(b + 8 - k, 8) if d == 0 else lax.rem(b + k, 8))
        slot = grads.at[t, rows(p if d == 0 else lax.rem(p + CHUNKS // 2, CHUNKS))]
        return remote(slot, slot, g_send.at[d, u], g_recv.at[d, u], ahead[d])

    def grad_arrival(d, u):
        k, p = lax.div(u, CHUNKS) + 1, lax.rem(u, CHUNKS)
        t = land(lax.rem(b + 8 - k, 8) if d == 0 else lax.rem(b + k, 8))
        slot = grads.at[t, rows(p if d == 0 else lax.rem(p + CHUNKS // 2, CHUNKS))]
        remote(slot, slot, g_send.at[d, u], g_recv.at[d, u], ahead[d]).wait_recv()

    def gelu_step(s, carry):
        r = lax.div(s, 2) + lax.rem(s, 2) * 2
        left = 10 + r
        right = 10 + lax.rem(r + 2, CHUNKS)
        sum_copy(0, right).wait_recv()
        sum_copy(1, left).wait_recv()
        x = total[rows(r), :] + taken[0, right].astype(jnp.float32) + taken[1, left].astype(jnp.float32)
        phi = 0.5 * (1.0 + lax.erf(x * inv_root_two))
        slope = phi + x * jnp.exp(-0.5 * x * x) * inv_root_tau
        act[rows(r), :] = (x * phi).astype(jnp.bfloat16)
        grads[group[7], rows(r), :] = (cot[rows(r), :].astype(jnp.float32) * slope).astype(jnp.bfloat16)
        grad_copy(0, r).start()
        grad_copy(1, lax.rem(r + 2, CHUNKS)).start()
        set_off(act_shift(r), shifted, act, act_mid, rows(r))
        return carry

    lax.fori_loop(0, CHUNKS, gelu_step, 0)

    def near_copy(z, h):
        return remote(near_out.at[z * 2 + h], near_in.at[z * 2 + h], n_send.at[z * 2 + h], n_recv.at[z * 2 + h], sibling)

    def far_copy(z, h):
        return remote(
            far_out.at[z * 2 + h], far_in.at[z * 2 + half], f_send.at[z * 2 + h], f_recv.at[z * 2 + half],
            at(gx=land(z), gy=h * 2 + core),
        )

    def far_own(z, h):
        return jnp.logical_and(land(z) == a, half == h)

    def back(t, r):
        return lax.dot_general(
            grads[t, rows(r), :], w_ref[...], (((1,), (1,)), ((), ())), preferred_element_type=jnp.float32
        )

    def give_near(z):
        def step(h, carry):
            near_out[z * 2 + h] = back(land(z), h * 2 + 1 - core).astype(jnp.bfloat16)
            near_copy(z, h).start()
            return carry

        lax.fori_loop(0, 2, step, 0)

    def weigh(z, first=False):
        t = land(z)

        def step(i, carry):
            columns = pl.ds(pl.multiple_of(i * 256, 256), 256)
            part = lax.dot_general(
                tokens[t, :, columns], grads[t], (((0,), (0,)), ((), ())), preferred_element_type=jnp.float32
            )
            total[columns, :] = part if first else total[columns, :] + part
            return carry

        lax.fori_loop(0, 3, step, 0)

    def give_far(z):
        def step(h, carry):
            value = back(land(z), h * 2 + core)
            near_copy(z, h).wait_recv()
            value = (value + near_in[z * 2 + h].astype(jnp.float32)).astype(jnp.bfloat16)

            @pl.when(far_own(z, h))
            def _():
                far_in[z * 2 + half] = value

            @pl.when(jnp.logical_not(far_own(z, h)))
            def _():
                far_out[z * 2 + h] = value
                far_copy(z, h).start()

            return carry

        lax.fori_loop(0, 2, step, 0)

    give_near(b)
    weigh(b, True)
    give_far(b)
    for k in (1, 2, 3):

        def forward(p, carry):
            for d in range(2):
                grad_arrival(d, (k - 1) * CHUNKS + p)
                grad_copy(d, k * CHUNKS + p).start()
            if k == 3:
                turn_act(p)
            return carry

        def keep(p, carry):
            for d in range(2):
                grad_arrival(d, (k - 1) * CHUNKS + p)
            return carry

        sent = CHUNKS if k < 3 else CHUNKS // 2
        lax.fori_loop(0, sent, forward, 0)
        lax.fori_loop(sent, CHUNKS, keep, 0)
        sides = lax.rem(b + 8 - k, 8), lax.rem(b + k, 8)
        for z in sides:
            give_near(z)
        for z in sides:
            weigh(z)
            give_far(z)

    def keep_last(p, carry):
        for d in range(2):
            grad_arrival(d, 3 * CHUNKS + p)
        turn_act(2 + p)
        return carry

    lax.fori_loop(0, CHUNKS // 2, keep_last, 0)
    opposite = lax.rem(b + 4, 8)
    give_near(opposite)
    give_far(opposite)
    weigh(opposite)

    def round_weight(i, carry):
        r = pl.ds(pl.multiple_of(i * 128, 128), 128)
        wg_ref[r, :] = total[r, :].astype(jnp.bfloat16)
        return carry

    lax.fori_loop(0, 6, round_weight, 0)

    def far_arrival(z, j):
        @pl.when(jnp.logical_not(far_own(z, j)))
        def _():
            slot = z * 2 + j
            remote(far_out.at[slot], far_in.at[slot], f_send.at[slot], f_recv.at[slot], sibling).wait_recv()

    def arrivals(z, carry):
        far_arrival(z, 0)
        far_arrival(z, 1)
        return carry

    lax.fori_loop(0, 8, arrivals, 0)

    def add_up(i, carry):
        r = pl.ds(pl.multiple_of(i * 16, 16), 16)
        value = far_in[0, r, :].astype(jnp.float32)
        for s in range(1, 16):
            value = value + far_in[s, r, :].astype(jnp.float32)
        ig_ref[r, :] = value.astype(jnp.bfloat16)
        return carry

    lax.fori_loop(0, piece // 16, add_up, 0)

    departed(cot_shift, shifted)
    for r in range(CHUNKS):
        arrived(act_turn(r), turned)
        departed(act_turn(r), turned)
        departed(act_shift(r), shifted)
        departed(cot_turn(r), turned)
    for s in range(2):
        for w in range(4):
            first_copy(s, w, False).wait_send()
        for e in range(4):
            for w in range(4):
                second_copy(s, e, w, False).wait_send()
                pass_copy(s, e, w, core).wait_send()

    def sent_sums(i, carry):
        for d in range(2):
            sum_copy(d, i).wait_send()
            grad_copy(d, i).wait_send()
        return carry

    lax.fori_loop(0, 14, sent_sums, 0)

    def sent_parts(z, carry):
        for h in range(2):
            near_copy(z, h).wait_send()

            @pl.when(jnp.logical_not(far_own(z, h)))
            def _():
                far_copy(z, h).wait_send()

        return carry

    lax.fori_loop(0, 8, sent_parts, 0)


def on_device(tokens, weight, cotangent):
    (piece, depth), (group, units) = tokens.shape, cotangent.shape
    bf16 = jnp.bfloat16
    shape = jax.ShapeDtypeStruct
    vmem = pl.BlockSpec(memory_space=pltpu.VMEM)
    dma = pltpu.SemaphoreType.DMA
    return pl.pallas_call(
        kernel,
        out_shape=(shape(cotangent.shape, bf16), shape(tokens.shape, bf16), shape(weight.shape, bf16)),
        in_specs=[vmem] * 3,
        out_specs=(vmem,) * 3,
        scratch_shapes=[
            pltpu.VMEM((8, group, depth), bf16),
            pltpu.VMEM((group, units), bf16),
            pltpu.VMEM((group, units), bf16),
            pltpu.VMEM((group, units), bf16),
            pltpu.VMEM((2, 14, piece, units), bf16),
            pltpu.VMEM((2, 14, piece, units), bf16),
            pltpu.VMEM((8, group, units), bf16),
            pltpu.VMEM((group, units), bf16),
            pltpu.VMEM((depth, units), jnp.float32),
            pltpu.VMEM((16, piece, depth), bf16),
            pltpu.VMEM((16, piece, depth), bf16),
            pltpu.VMEM((16, piece, depth), bf16),
            pltpu.VMEM((16, piece, depth), bf16),
            dma((40,)), dma((40,)), dma((32,)), dma((32,)),
            dma((14,)), dma((14,)),
            dma((2, 14)), dma((2, 14)), dma((2, 14)), dma((2, 14)),
            dma((16,)), dma((16,)), dma((16,)), dma((16,)),
        ],
        compiler_params=pltpu.CompilerParams(
            collective_id=0, has_side_effects=True, vmem_limit_bytes=60 * 1024 * 1024
        ),
    )(tokens, weight, cotangent)


def solution(mesh):
    in_specs = (P(("gx", "gy"), "gz"), P("gz", ("gy", "gx")), P("gx", ("gy", "gz")))
    out_specs = (P("gx", ("gy", "gz")), P(("gx", "gy"), "gz"), P("gz", ("gy", "gx")))
    return jax.shard_map(
        on_device, mesh=mesh, in_specs=in_specs, out_specs=out_specs, check_vma=False
    )
```

```python
import functools

import jax
import jax.numpy as jnp
from jax import lax
from jax.experimental import pallas as pl
from jax.experimental.pallas import tpu as pltpu
from jax.sharding import PartitionSpec as P

MESH = pl.DeviceIdType.MESH
inv_root_two = 0.7071067811865476
inv_root_tau = 0.3989422804014327

LANDING = (
    (2, 5, 4, 3, 6, 1, 0, 7),
    (1, 2, 7, 0, 5, 6, 3, 4),
    (0, 3, 6, 1, 4, 7, 2, 5),
    (7, 4, 5, 6, 3, 0, 1, 2),
    (6, 1, 0, 7, 2, 5, 4, 3),
    (5, 6, 3, 4, 1, 2, 7, 0),
    (4, 7, 2, 5, 0, 3, 6, 1),
    (3, 0, 1, 2, 7, 4, 5, 6),
)
Z_OF = tuple(tuple(LANDING[a].index(t) for t in range(8)) for a in range(8))
UNITS_OF = tuple(tuple([row[b] for row in LANDING].index(t) for b in range(8)) for t in range(8))
ORDER = (4, 3, 5, 2, 6, 1, 7, 0)
CHUNKS = 4


def choose(values, i):
    value = values[0]
    for k in range(1, len(values)):
        value = jnp.where(i == k, values[k], value)
    return value


def row_of(table, i):
    return choose([sum(v * 8**k for k, v in enumerate(row)) for row in table], i)


def entry(row, k):
    return lax.rem(lax.div(row, choose([8**p for p in range(8)], k)), 8)


def kernel(
    tok_ref, w_ref, cot_ref,
    act_ref, ig_ref, wg_ref,
    tokens, cot, cot_mid, act_mid, given, taken, grads, act, total, near_out, near_in, far_out, far_in,
    t_send, t_recv, s_send, s_recv, m_send, m_recv,
    r_send, r_recv, g_send, g_recv, n_send, n_recv, f_send, f_recv,
):
    a, q, b = lax.axis_index("gx"), lax.axis_index("gy"), lax.axis_index("gz")
    half, core = lax.div(q, 2), lax.rem(q, 2)
    piece = tok_ref.shape[0]
    rows = lambda r: pl.ds(pl.multiple_of(r * piece, piece), piece)
    at = lambda gx=a, gy=q, gz=b: {"gx": gx, "gy": gy, "gz": gz}
    up, down = lax.rem(b + 1, 8), lax.rem(b + 7, 8)
    sibling = at(gy=half * 2 + 1 - core)
    ahead = at(gx=a, gz=up), at(gx=a, gz=down)
    landings = row_of(LANDING, a)
    land = lambda z: entry(landings, z)
    units = entry(row_of(UNITS_OF, a), b)
    place_z = entry(row_of(Z_OF, b), a)
    turned, shifted = place_z != b, units != a
    x, y = half * 2 + lax.div(a, 4), lax.rem(a, 4)
    offset = [lax.rem(b + o, 8) for o in ORDER]
    group = [land(c) for c in offset]

    def remote(src, dst, send, recv, device):
        return pltpu.make_async_remote_copy(
            src_ref=src, dst_ref=dst, send_sem=send, recv_sem=recv, device_id=device, device_id_type=MESH
        )

    barrier = pltpu.get_barrier_semaphore()

    def greet(device):
        pl.semaphore_signal(barrier, inc=1, device_id=device, device_id_type=MESH)

    greet(at(gy=(1 - half) * 2 + core))
    greet(sibling)
    greet(ahead[0])
    greet(ahead[1])
    for c in range(1, 8):
        for j in range(2):
            greet(at(gx=lax.rem(a + c, 8), gy=j * 2 + core))

    @pl.when(turned)
    def _():
        greet(at(gz=place_z))
        greet(at(gz=units))

    pl.semaphore_wait(barrier, jnp.where(turned, 20, 18))

    side = piece // 2

    def spot(i, j, s, lo=0, n=side, of=core):
        px, py = lax.rem(x + i, 4), lax.rem(y + j, 4)
        row = (lax.div(px, 2) * 2 + of) * piece + s * side + lo
        return tokens.at[lax.rem(px, 2) * 4 + py, pl.ds(pl.multiple_of(row, side // 2), n)]

    def chip(i, j):
        px, py = lax.rem(x + i, 4), lax.rem(y + j, 4)
        return at(gx=lax.rem(px, 2) * 4 + py, gy=lax.div(px, 2) * 2 + core)

    def from_whom(w):
        return 1 if w in (0, 3) else 3

    def what(w):
        return ((1, 0, side), (3, 0, side), (2, 0, side // 2), (2, side // 2, side // 2))[w]

    def first_copy(s, w, arrival):
        e, lo, n = what(w)
        to = 4 - from_whom(w)
        if not arrival:
            e = (e + to) % 4
        slot = spot(e, 0, s, lo, n) if s == 0 else spot(0, e, s, lo, n)
        i = s * 4 + w
        return remote(slot, slot, t_send.at[i], t_recv.at[i], chip(to, 0) if s == 0 else chip(0, to))

    def second_copy(s, e, w, arrival):
        f, lo, n = what(w)
        to = 4 - from_whom(w)
        if not arrival:
            f = (f + to) % 4
        slot = spot(e, f, s, lo, n) if s == 0 else spot(f, e, s, lo, n)
        i = 8 + s * 16 + e * 4 + w
        return remote(slot, slot, t_send.at[i], t_recv.at[i], chip(0, to) if s == 0 else chip(to, 0))

    def pass_copy(s, e, f, of):
        slot = spot(e, f, s, of=of) if s == 0 else spot(f, e, s, of=of)
        i = s * 16 + e * 4 + f
        return remote(slot, slot, s_send.at[i], s_recv.at[i], sibling)

    def give_second(e):
        for s in range(2):
            second_copy(s, e, 0, False).start()
            second_copy(s, e, 1, False).start()
            pass_copy(s, e, 0, core).start()

    def relay_second(e):
        for s in range(2):
            for w in range(2):
                second_copy(s, e, w, True).wait_recv()
                second_copy(s, e, 3 - w, False).start()
                pass_copy(s, e, 1 + 2 * w, core).start()

    def end_second(e):
        for s in range(2):
            second_copy(s, e, 2, True).wait_recv()
            second_copy(s, e, 3, True).wait_recv()
            pass_copy(s, e, 2, core).start()

    cot_shift = remote(cot_mid, cot, m_send.at[1], m_recv.at[1], at(gx=units))

    def cot_turn(r):
        return remote(cot_ref.at[rows(r)], cot_mid.at[rows(r)], m_send.at[10 + r], m_recv.at[10 + r], at(gz=place_z))

    def act_shift(r):
        return remote(act.at[rows(r)], act_mid.at[rows(r)], m_send.at[2 + r], m_recv.at[2 + r], at(gx=land(b)))

    def act_turn(r):
        return remote(act_mid.at[rows(r)], act_ref.at[rows(r)], m_send.at[6 + r], m_recv.at[6 + r], at(gz=units))

    def set_off(copy, leaves, src, dst, r=slice(None)):
        @pl.when(leaves)
        def _():
            copy.start()

        @pl.when(jnp.logical_not(leaves))
        def _():
            dst[r, :] = src[r, :]

    def arrived(copy, leaves):
        @pl.when(leaves)
        def _():
            copy.wait_recv()

    def departed(copy, leaves):
        @pl.when(leaves)
        def _():
            copy.wait_send()

    def turn_act(r):
        arrived(act_shift(r), shifted)
        set_off(act_turn(r), turned, act_mid, act_ref, rows(r))

    def turn_cot(r):
        set_off(cot_turn(r), turned, cot_ref, cot_mid, rows(r))

    def gather_tokens():
        tokens[a, rows(q), :] = tok_ref[...]
        for s in range(2):
            first_copy(s, 0, False).start()
            first_copy(s, 1, False).start()
        give_second(0)
        for r in range(CHUNKS):
            turn_cot(r)
        for w in range(2):
            for s in range(2):
                first_copy(s, w, True).wait_recv()
                first_copy(s, 3 - w, False).start()
            give_second(1 + 2 * w)
        relay_second(0)
        for s in range(2):
            first_copy(s, 2, True).wait_recv()
            first_copy(s, 3, True).wait_recv()
        give_second(2)
        for e in (1, 3):
            relay_second(e)
        end_second(0)
        relay_second(2)
        for e in (1, 3, 2):
            end_second(e)
        for s in range(2):
            for e in range(4):
                for f in range(4):
                    pass_copy(s, e, f, 1 - core).wait_recv()

    def product(n, r):
        return jnp.dot(tokens[group[n], rows(r), :], w_ref[...], preferred_element_type=jnp.float32)

    def sum_copy(d, i):
        return remote(given.at[d, i], taken.at[d, i], r_send.at[d, i], r_recv.at[d, i], ahead[d])

    def place(d, p):
        return lax.rem(p + CHUNKS // 2, CHUNKS) if d == 0 else p

    def reduce_steps(first, last, base, n, add):
        def step(p, carry):
            i = base + p
            for d in range(2):
                value = product(n[d], place(d, p))
                if add:
                    sum_copy(d, i - CHUNKS).wait_recv()
                    value = value + taken[d, i - CHUNKS].astype(jnp.float32)
                given[d, i] = value.astype(jnp.bfloat16)
                sum_copy(d, i).start()
            return carry

        lax.fori_loop(first, last, step, 0)

    gather_tokens()
    reduce_steps(2, 4, -2, (0, 0), False)
    for k in (3, 2, 1):
        if k == 2:
            for r in range(CHUNKS):
                arrived(cot_turn(r), turned)
            set_off(cot_shift, shifted, cot_mid, cot)
        n = 7 - 2 * k
        base = (4 - k) * CHUNKS - 2
        if k == 3:
            reduce_steps(0, 2, base, (n, n + 1), False)
            reduce_steps(2, 4, base, (n, n + 1), True)
        else:
            reduce_steps(0, 4, base, (n, n + 1), True)

    def own_product(r, carry):
        total[rows(r), :] = product(7, r)
        return carry

    lax.fori_loop(0, CHUNKS, own_product, 0)

    arrived(cot_shift, shifted)

    def grad_copy(d, u):
        k, p = lax.div(u, CHUNKS), lax.rem(u, CHUNKS)
        t = land(lax.rem(b + 8 - k, 8) if d == 0 else lax.rem(b + k, 8))
        slot = grads.at[t, rows(p if d == 0 else lax.rem(p + CHUNKS // 2, CHUNKS))]
        return remote(slot, slot, g_send.at[d, u], g_recv.at[d, u], ahead[d])

    def grad_arrival(d, u):
        k, p = lax.div(u, CHUNKS) + 1, lax.rem(u, CHUNKS)
        t = land(lax.rem(b + 8 - k, 8) if d == 0 else lax.rem(b + k, 8))
        slot = grads.at[t, rows(p if d == 0 else lax.rem(p + CHUNKS // 2, CHUNKS))]
        remote(slot, slot, g_send.at[d, u], g_recv.at[d, u], ahead[d]).wait_recv()

    def gelu_step(s, carry):
        r = lax.div(s, 2) + lax.rem(s, 2) * 2
        left = 10 + r
        right = 10 + lax.rem(r + 2, CHUNKS)
        sum_copy(0, right).wait_recv()
        sum_copy(1, left).wait_recv()
        x = total[rows(r), :] + taken[0, right].astype(jnp.float32) + taken[1, left].astype(jnp.float32)
        phi = 0.5 * (1.0 + lax.erf(x * inv_root_two))
        slope = phi + x * jnp.exp(-0.5 * x * x) * inv_root_tau
        act[rows(r), :] = (x * phi).astype(jnp.bfloat16)
        grads[group[7], rows(r), :] = (cot[rows(r), :].astype(jnp.float32) * slope).astype(jnp.bfloat16)
        grad_copy(0, r).start()
        grad_copy(1, lax.rem(r + 2, CHUNKS)).start()
        set_off(act_shift(r), shifted, act, act_mid, rows(r))
        return carry

    lax.fori_loop(0, CHUNKS, gelu_step, 0)

    def near_copy(z, h):
        return remote(near_out.at[z * 2 + h], near_in.at[z * 2 + h], n_send.at[z * 2 + h], n_recv.at[z * 2 + h], sibling)

    def far_copy(z, h):
        return remote(
            far_out.at[z * 2 + h], far_in.at[z * 2 + half], f_send.at[z * 2 + h], f_recv.at[z * 2 + half],
            at(gx=land(z), gy=h * 2 + core),
        )

    def far_own(z, h):
        return jnp.logical_and(land(z) == a, half == h)

    def back(t, r):
        return lax.dot_general(
            grads[t, rows(r), :], w_ref[...], (((1,), (1,)), ((), ())), preferred_element_type=jnp.float32
        )

    def give_near(z):
        def step(h, carry):
            near_out[z * 2 + h] = back(land(z), h * 2 + 1 - core).astype(jnp.bfloat16)
            near_copy(z, h).start()
            return carry

        lax.fori_loop(0, 2, step, 0)

    def weigh(z, first=False):
        t = land(z)

        def step(i, carry):
            columns = pl.ds(pl.multiple_of(i * 256, 256), 256)
            part = lax.dot_general(
                tokens[t, :, columns], grads[t], (((0,), (0,)), ((), ())), preferred_element_type=jnp.float32
            )
            total[columns, :] = part if first else total[columns, :] + part
            return carry

        lax.fori_loop(0, 3, step, 0)

    def give_far(z):
        def step(h, carry):
            value = back(land(z), h * 2 + core)
            near_copy(z, h).wait_recv()
            value = (value + near_in[z * 2 + h].astype(jnp.float32)).astype(jnp.bfloat16)

            @pl.when(far_own(z, h))
            def _():
                far_in[z * 2 + half] = value

            @pl.when(jnp.logical_not(far_own(z, h)))
            def _():
                far_out[z * 2 + h] = value
                far_copy(z, h).start()

            return carry

        lax.fori_loop(0, 2, step, 0)

    give_near(b)
    weigh(b, True)
    give_far(b)
    for k in (1, 2, 3):

        def forward(p, carry):
            for d in range(2):
                grad_arrival(d, (k - 1) * CHUNKS + p)
                grad_copy(d, k * CHUNKS + p).start()
            if k == 3:
                turn_act(p)
            return carry

        def keep(p, carry):
            for d in range(2):
                grad_arrival(d, (k - 1) * CHUNKS + p)
            return carry

        sent = CHUNKS if k < 3 else CHUNKS // 2
        lax.fori_loop(0, sent, forward, 0)
        lax.fori_loop(sent, CHUNKS, keep, 0)
        sides = lax.rem(b + 8 - k, 8), lax.rem(b + k, 8)
        for z in sides:
            give_near(z)
        for z in sides:
            weigh(z)
            give_far(z)

    opposite = lax.rem(b + 4, 8)
    for p in range(2):
        for d in range(2):
            grad_arrival(d, 3 * CHUNKS + p)
        turn_act(2 + p)

        @pl.when(core != p)
        def _():
            give_near(opposite)

        @pl.when(core == p)
        def _():
            give_far(opposite)

    weigh(opposite)

    def round_weight(i, carry):
        r = pl.ds(pl.multiple_of(i * 128, 128), 128)
        wg_ref[r, :] = total[r, :].astype(jnp.bfloat16)
        return carry

    lax.fori_loop(0, 6, round_weight, 0)

    def far_arrival(z, j):
        @pl.when(jnp.logical_not(far_own(z, j)))
        def _():
            slot = z * 2 + j
            remote(far_out.at[slot], far_in.at[slot], f_send.at[slot], f_recv.at[slot], sibling).wait_recv()

    def arrivals(z, carry):
        far_arrival(z, 0)
        far_arrival(z, 1)
        return carry

    lax.fori_loop(0, 8, arrivals, 0)

    def add_up(i, carry):
        r = pl.ds(pl.multiple_of(i * 16, 16), 16)
        value = far_in[0, r, :].astype(jnp.float32)
        for s in range(1, 16):
            value = value + far_in[s, r, :].astype(jnp.float32)
        ig_ref[r, :] = value.astype(jnp.bfloat16)
        return carry

    lax.fori_loop(0, piece // 16, add_up, 0)

    departed(cot_shift, shifted)
    for r in range(CHUNKS):
        arrived(act_turn(r), turned)
        departed(act_turn(r), turned)
        departed(act_shift(r), shifted)
        departed(cot_turn(r), turned)
    for s in range(2):
        for w in range(4):
            first_copy(s, w, False).wait_send()
        for e in range(4):
            for w in range(4):
                second_copy(s, e, w, False).wait_send()
                pass_copy(s, e, w, core).wait_send()

    def sent_sums(i, carry):
        for d in range(2):
            sum_copy(d, i).wait_send()
            grad_copy(d, i).wait_send()
        return carry

    lax.fori_loop(0, 14, sent_sums, 0)

    def sent_parts(z, carry):
        for h in range(2):
            near_copy(z, h).wait_send()

            @pl.when(jnp.logical_not(far_own(z, h)))
            def _():
                far_copy(z, h).wait_send()

        return carry

    lax.fori_loop(0, 8, sent_parts, 0)


def on_device(tokens, weight, cotangent):
    (piece, depth), (group, units) = tokens.shape, cotangent.shape
    bf16 = jnp.bfloat16
    shape = jax.ShapeDtypeStruct
    vmem = pl.BlockSpec(memory_space=pltpu.VMEM)
    dma = pltpu.SemaphoreType.DMA
    return pl.pallas_call(
        kernel,
        out_shape=(shape(cotangent.shape, bf16), shape(tokens.shape, bf16), shape(weight.shape, bf16)),
        in_specs=[vmem] * 3,
        out_specs=(vmem,) * 3,
        scratch_shapes=[
            pltpu.VMEM((8, group, depth), bf16),
            pltpu.VMEM((group, units), bf16),
            pltpu.VMEM((group, units), bf16),
            pltpu.VMEM((group, units), bf16),
            pltpu.VMEM((2, 14, piece, units), bf16),
            pltpu.VMEM((2, 14, piece, units), bf16),
            pltpu.VMEM((8, group, units), bf16),
            pltpu.VMEM((group, units), bf16),
            pltpu.VMEM((depth, units), jnp.float32),
            pltpu.VMEM((16, piece, depth), bf16),
            pltpu.VMEM((16, piece, depth), bf16),
            pltpu.VMEM((16, piece, depth), bf16),
            pltpu.VMEM((16, piece, depth), bf16),
            dma((40,)), dma((40,)), dma((32,)), dma((32,)),
            dma((14,)), dma((14,)),
            dma((2, 14)), dma((2, 14)), dma((2, 14)), dma((2, 14)),
            dma((16,)), dma((16,)), dma((16,)), dma((16,)),
        ],
        compiler_params=pltpu.CompilerParams(
            collective_id=0, has_side_effects=True, vmem_limit_bytes=60 * 1024 * 1024
        ),
    )(tokens, weight, cotangent)


def solution(mesh):
    in_specs = (P(("gx", "gy"), "gz"), P("gz", ("gy", "gx")), P("gx", ("gy", "gz")))
    out_specs = (P("gx", ("gy", "gz")), P(("gx", "gy"), "gz"), P("gz", ("gy", "gx")))
    return jax.shard_map(
        on_device, mesh=mesh, in_specs=in_specs, out_specs=out_specs, check_vma=False
    )
```
